256 devices in a mesh: prow: 16 (over x, y), pcol: 16 (over z, core).
Axes of the slice: x: 4, y: 4, z: 8, core: 2. Of those that a mesh axis runs over, the one named last changes fastest.
Arguments:
- known_inverse: bfloat16 [32768, 16, 16, 128], P('prow', None, 'pcol'), may hold values from -6 to 6
- pattern: int32 [256, 16, 16, 1], P('prow', None, 'pcol'), may hold values 0 or 1
- panel_one: bfloat16 [32768, 512], P(('prow', 'pcol')), may hold values from -0.03125 to 0.03125
- panel_two: bfloat16 [32768, 512], P(('prow', 'pcol')), may hold values from -0.03125 to 0.03125
- panel_top: bfloat16 [512, 512], replicated, may hold values from -0.25 to 0.25
- structure: int32 [32768], P(('prow', 'pcol')), may hold values from 0 to 1, as said below
- diag_one: bfloat16 [512, 512], replicated, may hold values from -6 to 6
- diag_two: bfloat16 [512, 512], replicated, may hold values from -6 to 6
Outputs:
- inverse_one: bfloat16 [32768, 512], P(('prow', 'pcol'))
- corner_one: bfloat16 [512, 512], replicated
- inverse_top: bfloat16 [512, 512], replicated
- inverse_two: bfloat16 [32768, 512], P(('prow', 'pcol'))
- corner_two: bfloat16 [512, 512], replicated
The draws below stay inside these ranges and needn't reach their ends.
Inputs may be any that keep to these rules, and one draw needn't show every extreme that they name: `structure`: in every aligned pair of rows (2 k and 2 k + 1) at least one entry is 1.
All inputs are finite; a program needn't handle non-finite values. No bound on the sum of `pattern` on one device may be relied on, other than what follows from the above.
Results may differ from the reference program's by a relative error of at most 0.0058.
Values may be sent and summed in bfloat16 or wider, within the bound.
A program may use at most 128 MiB of HBM per device.

```python
import jax
import jax.numpy as jnp
from jax import lax

W = 512
BLK = 128
CB = 1
GRID_ROWS = 16
GRID_COLS = 16
C = 128
R = 32768
NB = 256


def draw_structure(key, part):
    choose = jax.random.randint(jax.random.fold_in(key, 71), (R // 2,), 0, 3)
    first = jnp.where(choose != 1, 1, 0)
    second = jnp.where(choose != 0, 1, 0)
    return jnp.stack([first, second], axis=1).reshape(R).astype(jnp.int32)


def place_ends(entries, stream_key, least, high):
    index_at = [jax.random.randint(jax.random.fold_in(stream_key, axis), (), 0, length) for axis, length in enumerate(entries.shape)]
    longest = entries.shape.index(max(entries.shape))
    neighbour = index_at[:longest] + [(index_at[longest] + 1) % entries.shape[longest]] + index_at[longest + 1:]
    return entries.at[tuple(index_at)].set(least).at[tuple(neighbour)].set(high)


def block_levels(rng, extent, shards, low, high):
    loudness, own = 1.0, jax.random.fold_in(rng, 6)
    for dim, parts in shards:
        heights = jnp.exp(jax.random.uniform(jax.random.fold_in(own, dim), (parts,), jnp.float32, low / len(shards), high / len(shards)))
        loudness = loudness * jnp.repeat(heights, extent[dim] // parts).reshape([-1 if axis == dim else 1 for axis in range(len(extent))])
    return loudness


def bell_draw(stream_key, extent, deviation, most, pieces=(), held_as=jnp.bfloat16):
    entries = deviation * jax.random.normal(stream_key, extent, jnp.float32)
    if pieces:
        entries = entries * block_levels(stream_key, extent, pieces, -0.22, 0.18)
    return jnp.clip(entries, -most, most).astype(held_as)


def setup_inputs(seed: int = 0) -> dict:
    arg_keys = jax.random.split(jax.random.key(seed), 9)
    known_inverse = bell_draw(arg_keys[0], (R, GRID_ROWS, GRID_COLS, C), 1.0, 6.0, ((0, 16), (2, 16)))
    pattern = place_ends((jax.random.randint(arg_keys[1], (NB, GRID_ROWS, GRID_COLS, CB), 0, 10) < 7).astype(jnp.int32), jax.random.fold_in(arg_keys[1], 1), 0, 1)
    panel_one = bell_draw(arg_keys[2], (R, W), R ** -0.5, 0.03125, ((0, 256),))
    panel_two = bell_draw(arg_keys[3], (R, W), R ** -0.5, 0.03125, ((0, 256),))
    panel_top = bell_draw(arg_keys[4], (W, W), W ** -0.5, 0.25)
    structure = draw_structure(jax.random.fold_in(arg_keys[8], 71), 0)
    diag_one = bell_draw(arg_keys[6], (W, W), 1.0, 6.0)
    diag_two = bell_draw(arg_keys[7], (W, W), 1.0, 6.0)
    return {"known_inverse": known_inverse, "pattern": pattern, "panel_one": panel_one, "panel_two": panel_two, "panel_top": panel_top, "structure": structure, "diag_one": diag_one, "diag_two": diag_two}


def masked_product(known_inverse, pattern, right_side):
    full_matrix = known_inverse.reshape(R, R)
    mark_table = pattern.reshape(NB, NB)
    group_blocks = NB // 16

    def one_group(group_index):
        row_block = lax.dynamic_slice_in_dim(full_matrix, (group_index * group_blocks * BLK).astype(jnp.int32), group_blocks * BLK, 0)
        flag_rows = lax.dynamic_slice_in_dim(mark_table, (group_index * group_blocks).astype(jnp.int32), group_blocks, 0)
        shaped = row_block.reshape(group_blocks, BLK, NB, BLK)
        kept_rows = jnp.where(flag_rows[:, None, :, None] > 0, shaped, jnp.zeros_like(shaped)).reshape(group_blocks * BLK, R)
        return jnp.dot(kept_rows, right_side, preferred_element_type=jnp.float32)

    stacked = lax.map(one_group, jnp.arange(16, dtype=jnp.int32))
    return stacked.reshape(R, right_side.shape[1])


def keep_rows(values, structure):
    return jnp.where(structure.reshape(R, 1) > 0, values, jnp.zeros_like(values))


def reference(known_inverse, pattern, panel_one, panel_two, panel_top, structure, diag_one, diag_two):
    masked_two = keep_rows(panel_two, structure)
    both_sums = masked_product(known_inverse, pattern, jnp.concatenate([panel_one, masked_two], axis=1))
    inverse_one = (-both_sums[:, :W]).astype(jnp.bfloat16)
    corner_full = diag_one.astype(jnp.float32) - jnp.dot(panel_one.T, inverse_one, preferred_element_type=jnp.float32)
    cross_sum = jnp.dot(inverse_one.T, masked_two, preferred_element_type=jnp.float32)
    top_value = jnp.dot(corner_full, panel_top.astype(jnp.float32), precision=lax.Precision.HIGHEST) + cross_sum
    inverse_top = (-top_value).astype(jnp.bfloat16)
    lower_two = -(both_sums[:, W:] + jnp.dot(inverse_one, panel_top, preferred_element_type=jnp.float32))
    inverse_two = keep_rows(lower_two, structure).astype(jnp.bfloat16)
    corner_two = diag_two.astype(jnp.float32) - jnp.dot(panel_top.T, inverse_top, preferred_element_type=jnp.float32) - jnp.dot(masked_two.T, inverse_two, preferred_element_type=jnp.float32)
    return inverse_one, corner_full.astype(jnp.bfloat16), inverse_top, inverse_two, corner_two.astype(jnp.bfloat16)
```

```python
import jax
import jax.numpy as jnp
from jax import lax
from jax.experimental import pallas as pl
from jax.experimental.pallas import tpu as pltpu
from jax.sharding import PartitionSpec as P

MESH = pl.DeviceIdType.MESH
BF = jnp.bfloat16
F32 = jnp.float32
CHUNKS = 4
HALF = 128
WIDE = 256
BLK = 128
W = 512


def dot(a, b):
    return jnp.dot(a, b, preferred_element_type=F32)


def dot_t(a, b):
    return lax.dot_general(a, b, (((0,), (0,)), ((), ())), preferred_element_type=F32)


def kernel(
    m_hbm, pat, p1, p2, ptop, struct, d1, d2,
    o_inv1, o_c1, o_top, o_inv2, o_c2,
    raw, tall, ms, g, keep, csnd, crcv, rsnd, rrcv, p2m, red, quad,
    ta, sa1, ra1, sa2, ra2, ra3, ga, gca,
    tb, sb1, rb1, sb2, rb2, rb3, gb, gcb,
    m_sem, ag1_sem, ag2_sem, agf_sem, ags_sem, c_sem, cs_sem, r_sem, rs_sem, ar_sem, ars_sem,
):
    me_r = lax.axis_index("prow")
    me_c = lax.axis_index("pcol")
    x, y, z, k = me_r // 4, me_r % 4, me_c // 2, me_c % 2
    other = 1 - k

    def at(dx, dy, dz, dk):
        return (
            ((x + dx) % 4) * 4 + (y + dy) % 4,
            ((z + dz) % 8) * 2 + (k + dk) % 2,
        )

    plane = [(dx, dy, 0, 0) for dx in range(4) for dy in range(4) if dx or dy]
    column = [(0, 0, dz, 0) for dz in range(1, 8)]
    mate = [(0, 0, 0, 1)]

    def send(src, dst, ssem, rsem, off):
        pltpu.make_async_remote_copy(
            src_ref=src, dst_ref=dst, send_sem=ssem, recv_sem=rsem,
            device_id=at(*off), device_id_type=MESH,
        ).start()

    def wait(ref, sem):
        pltpu.make_async_copy(ref, ref, sem).wait()

    def row_block(i):
        return 2 * i + other if i < 8 else 2 * (i - 8) + k

    for i in range(16):
        pltpu.make_async_copy(m_hbm.at[row_block(i)], raw.at[i], m_sem.at[i]).start()

    barrier = pltpu.get_barrier_semaphore()
    peers = plane + column + mate
    for off in peers:
        pl.semaphore_signal(barrier, inc=1, device_id=at(*off), device_id_type=MESH)

    flags = jnp.broadcast_to(struct[...], (BLK, BLK)) > 0
    eye = lax.broadcasted_iota(jnp.int32, (BLK, BLK), 0) == lax.broadcasted_iota(
        jnp.int32, (BLK, BLK), 1
    )
    pick = jnp.where(flags & eye, 1.0, 0.0).astype(BF)
    p2m[...] = dot(pick, p2[...]).astype(BF)
    for s in range(CHUNKS):
        for h in range(2):
            src = p1 if s < 2 else p2m
            c0 = (s % 2) * WIDE + h * HALF
            g[s, h, x, y] = src[:, c0 : c0 + HALF]

    pl.semaphore_wait(barrier, len(peers))

    def step_along(h, first):
        along_x = (h == 0) == first
        return (lambda d: (d, 0, 0, 0)) if along_x else (lambda d: (0, d, 0, 0))

    def gather1(s):
        for h in range(2):
            off = step_along(h, True)
            blk = g.at[s, h, x, y]
            for d in (1, 3, 2):
                send(blk, blk, ags_sem.at[s, h], ag1_sem.at[s, h], off(d))

    def line(s, h, d, lo, n):
        if h == 0:
            return g.at[s, h, pl.ds(lo, n), (y + d) % 4]
        return g.at[s, h, (x + d) % 4, pl.ds(lo, n)]

    def gather2(s):
        for h in range(2):
            wait(line(s, h, 0, 0, 3), ag1_sem.at[s, h])
            off = step_along(h, False)
            mine = line(s, h, 0, 0, 4)
            send(mine, mine, ags_sem.at[s, h], ag2_sem.at[s, h, 0], off(1))
            send(mine, mine, ags_sem.at[s, h], ag2_sem.at[s, h, 1], off(3))

    def gather3(s):
        for h in range(2):
            off = step_along(h, False)
            wait(line(s, h, 3, 0, 4), ag2_sem.at[s, h, 0])
            low = line(s, h, 3, 0, 2)
            send(low, low, ags_sem.at[s, h], agf_sem.at[s, h], off(1))
            wait(line(s, h, 1, 0, 4), ag2_sem.at[s, h, 1])
            high = line(s, h, 1, 2, 2)
            send(high, high, ags_sem.at[s, h], agf_sem.at[s, h], off(3))

    def gathered(s):
        for h in range(2):
            wait(line(s, h, 2, 0, 4), agf_sem.at[s, h])

    def relayout(lo, hi):
        @pl.loop(lo, hi)
        def _(i):
            rb = jnp.where(i < 8, 2 * i + other, 2 * (i - 8) + k)
            pltpu.make_async_copy(m_hbm.at[rb], raw.at[i], m_sem.at[i]).wait()
            tall[...] = raw[i].astype(F32)
            for a in range(16):
                v = tall[pl.ds(a, BLK, stride=16), :]
                v = jnp.where(pat[rb, a] > 0, v, 0.0)
                ms[pl.ds(i * BLK, BLK), a * BLK : (a + 1) * BLK] = v.astype(BF)

    def panel(s):
        return jnp.concatenate([g[s, h].reshape(2048, HALF) for h in range(2)], axis=1)

    def product(s, tile):
        acc = dot(ms[tile * 1024 : (tile + 1) * 1024, :], panel(s)).reshape(8, BLK, WIDE)
        if tile == 0:
            csnd[s] = acc.astype(BF)
            send(csnd.at[s], crcv.at[s], cs_sem.at[s], c_sem.at[s], mate[0])
        else:
            keep[s] = acc

    def cores(s):
        wait(crcv.at[s], c_sem.at[s])

    def own(s, b, h):
        c = slice(h * HALF, (h + 1) * HALF)
        return keep[s, b, :, c] + crcv[s, b, :, c].astype(F32)

    def slots(t):
        return (0, 1) if t == 1 else (2 * t - 3, 2)

    def ring(s, t):
        for way in range(2):
            if t > 1:
                lo, n = slots(t - 1)
                wait(rrcv.at[s, way, pl.ds(lo, n)], r_sem.at[s, way, t - 2])
        if t == 5:
            for h in range(2):
                red[s, h] = own(s, z, h) + rrcv[s, 0, 5 + h].astype(F32) + rrcv[s, 1, 5 + h].astype(F32)
            return
        for way in range(2):
            d = 5 - t if way == 0 else 8 - (5 - t)
            b = (z + d) % 8
            lo, n = slots(t)
            for h in range(2):
                if t == 1:
                    if h == way:
                        rsnd[s, way, 0] = own(s, b, h).astype(BF)
                    continue
                v = own(s, b, h)
                if t > 2:
                    v = v + rrcv[s, way, slots(t - 1)[0] + h].astype(F32)
                elif h == way:
                    v = v + rrcv[s, way, 0].astype(F32)
                rsnd[s, way, lo + h] = v.astype(BF)
            send(
                rsnd.at[s, way, pl.ds(lo, n)], rrcv.at[s, way, pl.ds(lo, n)],
                rs_sem.at[s], r_sem.at[s, way, t - 1], (0, 0, 1 if way == 0 else 7, 0),
            )

    def sum1(q, t32, s1, r1):
        s1[...] = t32[:, pl.ds(pl.multiple_of(other * 256, 256), 256), :].astype(BF)
        send(s1, r1, ars_sem.at[q, 0], ar_sem.at[q, 0], mate[0])

    def sum2(q, t32, r1, s2, r2):
        wait(r1, ar_sem.at[q, 0])
        n = t32.shape[0]
        for m in range(n):
            v = t32[m, pl.ds(pl.multiple_of(k * 256, 256), 256), :] + r1[m].astype(F32)
            s2[:, m] = v.astype(BF).reshape(16, 16, W)
        for off in plane:
            j = ((x + off[0]) % 4) * 4 + (y + off[1]) % 4
            send(s2.at[j], r2.at[me_r], ars_sem.at[q, 1], ar_sem.at[q, 1], off)
        r2[me_r] = s2[me_r]

    def sum3(q, r2, r3):
        wait(r2.at[pl.ds(0, 15)], ar_sem.at[q, 1])
        v = r2[0].astype(F32)
        for j in range(1, 16):
            v = v + r2[j].astype(F32)
        r3[z] = v.astype(BF)
        for off in column:
            send(r3.at[z], r3.at[z], ars_sem.at[q, 2], ar_sem.at[q, 2], off)

    def sum4(q, r3):
        wait(r3.at[pl.ds(0, 7)], ar_sem.at[q, 2])
        v = r3[0].astype(F32)
        for j in range(1, 8):
            v = v + r3[j].astype(F32)
        return v

    def spread(q, ga_):
        for off in plane:
            send(ga_.at[me_r], ga_.at[me_r], ars_sem.at[q, 3], ar_sem.at[q, 3], off)

    def swap(q, ga_, gc_):
        wait(ga_.at[pl.ds(0, 15)], ar_sem.at[q, 3])
        send(ga_, gc_, ars_sem.at[q, 4], ar_sem.at[q, 4], mate[0])

    def lay(out, ga_, gc_, m):
        out[pl.ds(pl.multiple_of(k * 256, 256), 256), :] = ga_[:, m].reshape(256, W)
        out[pl.ds(pl.multiple_of(other * 256, 256), 256), :] = gc_[:, m].reshape(256, W)

    my_rows = pl.ds(pl.multiple_of(k * 256 + me_r * 16, 16), 16)

    def first_rows():
        r = jnp.concatenate(
            [jnp.concatenate([red[s, h] for h in range(2)], axis=1) for s in range(2)], axis=1
        )
        o_inv1[...] = (-r).astype(BF)
        ta[0] = dot_t(p1[...], o_inv1[...])
        ta[1] = dot_t(o_inv1[...], p2m[...])
        sum1(0, ta, sa1, ra1)

    def second_rows():
        r = jnp.concatenate(
            [jnp.concatenate([red[s, h] for h in range(2)], axis=1) for s in range(2, 4)], axis=1
        )
        low = -(r + dot(o_inv1[...], ptop[...]))
        kept = dot(pick, jnp.ones((BLK, W), BF)) > 0.5
        o_inv2[...] = jnp.where(kept, low, 0.0).astype(BF)
        tb[0] = dot_t(p2m[...], o_inv2[...])
        sum1(1, tb, sb1, rb1)

    def first_corner():
        v = sum4(0, ra3)
        s1 = d1[my_rows, :].astype(F32) - v[0]
        hi = s1.astype(BF)
        rest = s1 - hi.astype(F32)
        mid = rest.astype(BF)
        low = (rest - mid.astype(F32)).astype(BF)
        t = ptop[...]
        top = dot(hi, t) + (dot(mid, t) + dot(low, t))
        ga[me_r, 0] = hi
        ga[me_r, 1] = (-(top + v[1])).astype(BF)
        spread(0, ga)

    def first_done():
        wait(gca, ar_sem.at[0, 4])
        lay(o_c1, ga, gca, 0)
        lay(o_top, ga, gca, 1)
        quad[...] = dot_t(ptop[...], o_top[...])

    def second_corner():
        v = sum4(1, rb3)
        gb[me_r, 0] = (d2[my_rows, :].astype(F32) - quad[my_rows, :] - v[0]).astype(BF)
        spread(1, gb)

    gather1(0)
    gather1(1)
    relayout(0, 4)
    gather2(0)
    gather1(2)
    relayout(4, 9)
    gather2(1)
    relayout(9, 16)
    gather3(0)
    gather2(2)
    gather1(3)
    gathered(0)
    product(0, 0)
    gather3(1)
    product(0, 1)
    gather2(3)
    cores(0)
    ring(0, 1)
    gathered(1)
    product(1, 0)
    ring(0, 2)
    gather3(2)
    product(1, 1)
    ring(0, 3)
    cores(1)
    ring(1, 1)
    gathered(2)
    product(2, 0)
    ring(0, 4)
    ring(1, 2)
    gather3(3)
    product(2, 1)
    ring(0, 5)
    ring(1, 3)
    cores(2)
    ring(2, 1)
    gathered(3)
    product(3, 0)
    ring(1, 4)
    ring(2, 2)
    product(3, 1)
    cores(3)
    ring(3, 1)
    ring(1, 5)
    first_rows()
    ring(2, 3)
    ring(3, 2)
    sum2(0, ta, ra1, sa2, ra2)
    ring(2, 4)
    ring(3, 3)
    sum3(0, ra2, ra3)
    ring(2, 5)
    ring(3, 4)
    first_corner()
    ring(3, 5)
    second_rows()
    swap(0, ga, gca)
    sum2(1, tb, rb1, sb2, rb2)
    first_done()
    sum3(1, rb2, rb3)
    second_corner()
    swap(1, gb, gcb)

    for s in range(CHUNKS):
        for h in range(2):
            wait(raw.at[0, pl.ds(0, 15 * BLK)], ags_sem.at[s, h])
        wait(csnd.at[s], cs_sem.at[s])
        wait(rsnd.at[s], rs_sem.at[s])
    for q, s1, s2, r3, g_ in ((0, sa1, sa2, ra3, ga), (1, sb1, sb2, rb3, gb)):
        wait(s1, ars_sem.at[q, 0])
        wait(s2.at[pl.ds(0, 15)], ars_sem.at[q, 1])
        wait(r3.at[pl.ds(0, 7)], ars_sem.at[q, 2])
        wait(g_.at[pl.ds(0, 15)], ars_sem.at[q, 3])
        wait(g_, ars_sem.at[q, 4])
    wait(gcb, ar_sem.at[1, 4])
    lay(o_c2, gb, gcb, 0)


def on_device(known_inverse, pattern, panel_one, panel_two, panel_top, structure, diag_one, diag_two):
    vm, sm, hbm = (pl.BlockSpec(memory_space=s) for s in (pltpu.VMEM, pltpu.SMEM, pl.ANY))
    V, S = pltpu.VMEM, pltpu.SemaphoreType.DMA

    def sums(n, no):
        return [
            V((n, W, W), F32),
            V((n, 256, W), BF), V((n, 256, W), BF),
            V((16, n, 16, W), BF), V((16, n, 16, W), BF),
            V((8, n, 16, W), BF),
            V((16, no, 16, W), BF), V((16, no, 16, W), BF),
        ]

    corner = jax.ShapeDtypeStruct((W, W), BF)
    rows = jax.ShapeDtypeStruct((BLK, W), BF)
    return pl.pallas_call(
        kernel,
        out_shape=(rows, corner, corner, rows, corner),
        in_specs=[hbm, sm, vm, vm, vm, vm, vm, vm],
        out_specs=(vm,) * 5,
        scratch_shapes=[
            V((16, 2048, BLK), BF), V((2048, BLK), F32), V((2048, 2048), BF),
            V((CHUNKS, 2, 4, 4, BLK, HALF), BF),
            V((CHUNKS, 8, BLK, WIDE), F32), V((CHUNKS, 8, BLK, WIDE), BF), V((CHUNKS, 8, BLK, WIDE), BF),
            V((CHUNKS, 2, 7, BLK, HALF), BF), V((CHUNKS, 2, 7, BLK, HALF), BF),
            V((BLK, W), BF), V((CHUNKS, 2, BLK, HALF), F32), V((W, W), F32),
            *sums(2, 2), *sums(1, 1),
            S((16,)), S((CHUNKS, 2)), S((CHUNKS, 2, 2)), S((CHUNKS, 2)), S((CHUNKS, 2)),
            S((CHUNKS,)), S((CHUNKS,)), S((CHUNKS, 2, 4)), S((CHUNKS,)), S((2, 5)), S((2, 5)),
        ],
        compiler_params=pltpu.CompilerParams(
            collective_id=0, has_side_effects=True, vmem_limit_bytes=60 * 2**20
        ),
        cost_estimate=pl.CostEstimate(flops=2 * 2048 * 2048 * 1024, bytes_accessed=12 * 2**20, transcendentals=0),
        name="inverse",
    )(
        known_inverse.reshape(16, 2048, BLK),
        pattern.reshape(16, 16),
        panel_one, panel_two, panel_top, structure.reshape(1, BLK), diag_one, diag_two,
    )


def solution(mesh):
    in_specs = (
        P("prow", None, "pcol", None), P("prow", None, "pcol", None),
        P(("prow", "pcol"), None), P(("prow", "pcol"), None),
        P(), P(("prow", "pcol")), P(), P(),
    )
    out_specs = (P(("prow", "pcol"), None), P(), P(), P(("prow", "pcol"), None), P())
    return jax.shard_map(on_device, mesh=mesh, in_specs=in_specs, out_specs=out_specs, check_vma=False)
```

```python
import jax
import jax.numpy as jnp
from jax import lax
from jax.experimental import pallas as pl
from jax.experimental.pallas import tpu as pltpu
from jax.sharding import PartitionSpec as P

MESH = pl.DeviceIdType.MESH
BF = jnp.bfloat16
F32 = jnp.float32
CHUNKS = 4
HALF = 128
WIDE = 256
BLK = 128
W = 512


def dot(a, b):
    return jnp.dot(a, b, preferred_element_type=F32)


def dot_t(a, b):
    return lax.dot_general(a, b, (((0,), (0,)), ((), ())), preferred_element_type=F32)


def kernel(
    m_hbm, pat, p1, p2, ptop, struct, d1, d2,
    o_inv1, o_c1, o_top, o_inv2, o_c2,
    raw, tall, ms, g, zg, keep, csnd, crcv, rsnd, rrcv, red, base,
    ta, sa1, ra1, sa2, ra2, ra3, ga, gca,
    tb, sb, rb, sc, rc, gb, gcb,
    m_sem, ag1_sem, ag2_sem, agf_sem, ags_sem, zg_sem, zs_sem, c_sem, cs_sem, r_sem, rs_sem, ar_sem, ars_sem, br_sem, bs_sem,
):
    me_r = lax.axis_index("prow")
    me_c = lax.axis_index("pcol")
    x, y, z, k = me_r // 4, me_r % 4, me_c // 2, me_c % 2
    other = 1 - k

    def at(dx, dy, dz, dk):
        return (
            ((x + dx) % 4) * 4 + (y + dy) % 4,
            ((z + dz) % 8) * 2 + (k + dk) % 2,
        )

    plane = [(dx, dy, 0, 0) for dx in range(4) for dy in range(4) if dx or dy]
    column = [(0, 0, dz, 0) for dz in range(1, 8)]
    mate = [(0, 0, 0, 1)]
    tower = [(0, 0, dz, dk) for dk in (0, 1) for dz in range(8) if dz or dk]

    def send(src, dst, ssem, rsem, off):
        pltpu.make_async_remote_copy(
            src_ref=src, dst_ref=dst, send_sem=ssem, recv_sem=rsem,
            device_id=at(*off), device_id_type=MESH,
        ).start()

    def wait(ref, sem):
        pltpu.make_async_copy(ref, ref, sem).wait()

    def row_block(i):
        return 2 * i + other if i < 8 else 2 * (i - 8) + k

    for i in range(16):
        pltpu.make_async_copy(m_hbm.at[row_block(i)], raw.at[i], m_sem.at[i]).start()

    barrier = pltpu.get_barrier_semaphore()
    peers = plane + tower
    for off in peers:
        pl.semaphore_signal(barrier, inc=1, device_id=at(*off), device_id_type=MESH)

    flags = jnp.broadcast_to(struct[...], (BLK, BLK)) > 0
    eye = lax.broadcasted_iota(jnp.int32, (BLK, BLK), 0) == lax.broadcasted_iota(
        jnp.int32, (BLK, BLK), 1
    )
    pick = jnp.where(flags & eye, 1.0, 0.0).astype(BF)
    zg[0, z] = p1[...]
    zg[1, z] = dot(pick, p2[...]).astype(BF)
    for s in range(2):
        for h in range(2):
            c0 = s * WIDE + h * HALF
            g[s, h, x, y] = p1[:, c0 : c0 + HALF]

    pl.semaphore_wait(barrier, len(peers))

    def step_along(h, first):
        along_x = (h == 0) == first
        return (lambda d: (d, 0, 0, 0)) if along_x else (lambda d: (0, d, 0, 0))

    def gather1(s):
        for h in range(2):
            off = step_along(h, True)
            blk = g.at[s, h, x, y]
            for d in (1, 3, 2):
                send(blk, blk, ags_sem.at[s, h], ag1_sem.at[s, h], off(d))

    def line(s, h, d, lo, n):
        if h == 0:
            return g.at[s, h, pl.ds(lo, n), (y + d) % 4]
        return g.at[s, h, (x + d) % 4, pl.ds(lo, n)]

    def gather2(s):
        for h in range(2):
            wait(line(s, h, 0, 0, 3), ag1_sem.at[s, h])
            off = step_along(h, False)
            mine = line(s, h, 0, 0, 4)
            send(mine, mine, ags_sem.at[s, h], ag2_sem.at[s, h, 0], off(1))
            send(mine, mine, ags_sem.at[s, h], ag2_sem.at[s, h, 1], off(3))

    def gather3(s):
        for h in range(2):
            off = step_along(h, False)
            wait(line(s, h, 3, 0, 4), ag2_sem.at[s, h, 0])
            low = line(s, h, 3, 0, 2)
            send(low, low, ags_sem.at[s, h], agf_sem.at[s, h], off(1))
            wait(line(s, h, 1, 0, 4), ag2_sem.at[s, h, 1])
            high = line(s, h, 1, 2, 2)
            send(high, high, ags_sem.at[s, h], agf_sem.at[s, h], off(3))

    def gathered(s):
        for h in range(2):
            wait(line(s, h, 2, 0, 4), agf_sem.at[s, h])

    def second_panel():
        v = zg[1, z].astype(F32) - dot(p1[...], ptop[...])
        for s in range(2, CHUNKS):
            for h in range(2):
                c0 = (s - 2) * WIDE + h * HALF
                g[s, h, x, y] = v[:, c0 : c0 + HALF].astype(BF)

    def rows_along(t, p):
        for way in range(2):
            d = t - 1 if way else -(t - 1)
            blk = zg.at[p, (z + d + 8) % 8]
            half = blk.at[pl.ds(64 * way, 64)]
            if t > 1:
                got = half if t == 5 else blk
                wait(got, zg_sem.at[p, way, t - 2])
            if t == 5:
                continue
            src = half if t == 4 else blk
            send(src, src, zs_sem.at[p], zg_sem.at[p, way, t - 1], (0, 0, 7 if way else 1, 0))

    def relayout(lo, hi):
        @pl.loop(lo, hi)
        def _(i):
            rb = jnp.where(i < 8, 2 * i + other, 2 * (i - 8) + k)
            pltpu.make_async_copy(m_hbm.at[rb], raw.at[i], m_sem.at[i]).wait()
            tall[...] = raw[i].astype(F32)
            for a in range(16):
                v = tall[pl.ds(a, BLK, stride=16), :]
                v = jnp.where(pat[rb, a] > 0, v, 0.0)
                ms[pl.ds(i * BLK, BLK), a * BLK : (a + 1) * BLK] = v.astype(BF)

    def panel(s):
        return jnp.concatenate([g[s, h].reshape(2048, HALF) for h in range(2)], axis=1)

    def product(s, tile):
        acc = dot(ms[tile * 1024 : (tile + 1) * 1024, :], panel(s)).reshape(8, BLK, WIDE)
        if tile == 0:
            csnd[s] = acc.astype(BF)
            send(csnd.at[s], crcv.at[s], cs_sem.at[s], c_sem.at[s], mate[0])
        else:
            keep[s] = acc

    def cores(s):
        wait(crcv.at[s], c_sem.at[s])
        keep[s] = keep[s] + crcv[s].astype(F32)

    def part(s):
        v = keep[s].astype(BF).reshape(1024, WIDE)
        c = slice((s % 2) * WIDE, (s % 2 + 1) * WIDE)
        two = zg[1].reshape(1024, W)
        if s < 2:
            ta[0, :, c] = dot_t(zg[0].reshape(1024, W), v)
            ta[1, c, :] = dot_t(v, two)
        else:
            tb[s - 2] = tb[s - 2] + dot_t(two, v)

    def own(s, b, h):
        c = slice(h * HALF, (h + 1) * HALF)
        return keep[s, b, :, c]

    def slots(t):
        return (0, 1) if t == 1 else (2 * t - 3, 2)

    def ring(s, t):
        for way in range(2):
            if t > 1:
                lo, n = slots(t - 1)
                wait(rrcv.at[s, way, pl.ds(lo, n)], r_sem.at[s, way, t - 2])
        if t == 5:
            for h in range(2):
                red[s, h] = own(s, z, h) + rrcv[s, 0, 5 + h].astype(F32) + rrcv[s, 1, 5 + h].astype(F32)
            return
        for way in range(2):
            d = 5 - t if way == 0 else 8 - (5 - t)
            b = (z + d) % 8
            lo, n = slots(t)
            for h in range(2):
                if t == 1:
                    if h == way:
                        rsnd[s, way, 0] = own(s, b, h).astype(BF)
                    continue
                v = own(s, b, h)
                if t > 2:
                    v = v + rrcv[s, way, slots(t - 1)[0] + h].astype(F32)
                elif h == way:
                    v = v + rrcv[s, way, 0].astype(F32)
                rsnd[s, way, lo + h] = v.astype(BF)
            send(
                rsnd.at[s, way, pl.ds(lo, n)], rrcv.at[s, way, pl.ds(lo, n)],
                rs_sem.at[s], r_sem.at[s, way, t - 1], (0, 0, 1 if way == 0 else 7, 0),
            )

    def sum1(q, t32, s1, r1):
        s1[...] = t32[:, pl.ds(pl.multiple_of(other * 256, 256), 256), :].astype(BF)
        send(s1, r1, ars_sem.at[q, 0], ar_sem.at[q, 0], mate[0])

    def sum2(q, t32, r1, s2, r2):
        wait(r1, ar_sem.at[q, 0])
        n = t32.shape[0]
        for m in range(n):
            v = t32[m, pl.ds(pl.multiple_of(k * 256, 256), 256), :] + r1[m].astype(F32)
            s2[:, m] = v.astype(BF).reshape(16, 16, W)
        for off in plane:
            j = ((x + off[0]) % 4) * 4 + (y + off[1]) % 4
            send(s2.at[j], r2.at[me_r], ars_sem.at[q, 1], ar_sem.at[q, 1], off)
        r2[me_r] = s2[me_r]

    def sum3(q, r2, r3):
        wait(r2.at[pl.ds(0, 15)], ar_sem.at[q, 1])
        v = r2[0].astype(F32)
        for j in range(1, 16):
            v = v + r2[j].astype(F32)
        r3[z] = v.astype(BF)
        for off in column:
            send(r3.at[z], r3.at[z], ars_sem.at[q, 2], ar_sem.at[q, 2], off)

    def sum4(q, r3):
        wait(r3.at[pl.ds(0, 7)], ar_sem.at[q, 2])
        v = r3[0].astype(F32)
        for j in range(1, 8):
            v = v + r3[j].astype(F32)
        return v

    def spread(q, ga_):
        for off in plane:
            send(ga_.at[me_r], ga_.at[me_r], ars_sem.at[q, 3], ar_sem.at[q, 3], off)

    def swap(q, ga_, gc_):
        wait(ga_.at[pl.ds(0, 15)], ar_sem.at[q, 3])
        send(ga_, gc_, ars_sem.at[q, 4], ar_sem.at[q, 4], mate[0])

    def lay(out, ga_, gc_, m):
        out[pl.ds(pl.multiple_of(k * 256, 256), 256), :] = ga_[:, m].reshape(256, W)
        out[pl.ds(pl.multiple_of(other * 256, 256), 256), :] = gc_[:, m].reshape(256, W)

    my_rows = pl.ds(pl.multiple_of(k * 256 + me_r * 16, 16), 16)

    def first_rows():
        r = jnp.concatenate(
            [jnp.concatenate([red[s, h] for h in range(2)], axis=1) for s in range(2)], axis=1
        )
        o_inv1[...] = (-r).astype(BF)

    def second_rows():
        r = jnp.concatenate(
            [jnp.concatenate([red[s, h] for h in range(2)], axis=1) for s in range(2, 4)], axis=1
        )
        kept = dot(pick, jnp.ones((BLK, W), BF)) > 0.5
        o_inv2[...] = jnp.where(kept, -r, 0.0).astype(BF)

    def first_corner():
        v = sum4(0, ra3)
        s1 = d1[my_rows, :].astype(F32) + v[0]
        hi = s1.astype(BF)
        rest = s1 - hi.astype(F32)
        mid = rest.astype(BF)
        low = (rest - mid.astype(F32)).astype(BF)
        t = ptop[...]
        top = dot(hi, t) + (dot(mid, t) + dot(low, t))
        ga[me_r, 0] = hi
        ga[me_r, 1] = (v[1] - top).astype(BF)
        spread(0, ga)

    def first_done():
        wait(gca, ar_sem.at[0, 4])
        lay(o_c1, ga, gca, 0)
        lay(o_top, ga, gca, 1)

    def fixed_part():
        t = ptop[...]
        base[...] = d2[...].astype(F32) + dot_t(t, dot(d1[...], t).astype(BF))

    def first_part():
        t = ptop[...]
        u = dot_t(t, (dot(ta[0].astype(BF), t) - ta[1]).astype(BF))
        tb[0] = u[:, :WIDE]
        tb[1] = u[:, WIDE:]

    def low1(c):
        for half in range(2):
            sb[c, :, half] = tb[c, half * 256 : (half + 1) * 256].astype(BF).reshape(16, 16, WIDE)
        for off in plane:
            j = ((x + off[0]) % 4) * 4 + (y + off[1]) % 4
            send(sb.at[c, j], rb.at[c, me_r], bs_sem.at[c, 0], br_sem.at[c, 0], off)
        rb[c, me_r] = sb[c, me_r]

    def low2(c):
        wait(rb.at[c, pl.ds(0, 15)], br_sem.at[c, 0])
        v = rb[c, 0].astype(F32)
        for j in range(1, 16):
            v = v + rb[c, j].astype(F32)
        sc[c] = v.astype(BF)
        for off in tower:
            to = k if off[3] == 0 else other
            send(sc.at[c, to], rc.at[c, me_c], bs_sem.at[c, 1], br_sem.at[c, 1], off)
        rc[c, me_c] = sc[c, k]

    def low3(c):
        wait(rc.at[c, pl.ds(0, 15)], br_sem.at[c, 1])
        v = base[my_rows, c * WIDE : (c + 1) * WIDE]
        for j in range(16):
            v = v + rc[c, j].astype(F32)
        gb[c, me_r] = v.astype(BF)
        for off in plane:
            send(gb.at[c, me_r], gb.at[c, me_r], bs_sem.at[c, 2], br_sem.at[c, 2], off)

    def low4(c):
        wait(gb.at[c, pl.ds(0, 15)], br_sem.at[c, 2])
        send(gb.at[c], gcb.at[c], bs_sem.at[c, 3], br_sem.at[c, 3], mate[0])

    def low5(c):
        wait(gcb.at[c], br_sem.at[c, 3])
        cols = slice(c * WIDE, (c + 1) * WIDE)
        o_c2[pl.ds(pl.multiple_of(k * 256, 256), 256), cols] = gb[c].reshape(256, WIDE)
        o_c2[pl.ds(pl.multiple_of(other * 256, 256), 256), cols] = gcb[c].reshape(256, WIDE)

    gather1(0)
    rows_along(1, 0)
    gather1(1)
    rows_along(1, 1)
    second_panel()
    relayout(0, 3)
    gather2(0)
    rows_along(2, 0)
    relayout(3, 5)
    gather2(1)
    gather1(2)
    relayout(5, 9)
    rows_along(2, 1)
    relayout(9, 12)
    rows_along(3, 0)
    gather3(0)
    gather2(2)
    gather1(3)
    relayout(12, 16)
    rows_along(3, 1)
    gather3(1)
    gather2(3)
    gathered(0)
    product(0, 0)
    rows_along(4, 0)
    gather3(2)
    product(0, 1)
    rows_along(4, 1)
    gathered(1)
    product(1, 0)
    gather3(3)
    cores(0)
    ring(0, 1)
    product(1, 1)
    rows_along(5, 0)
    rows_along(5, 1)
    part(0)
    cores(1)
    part(1)
    sum1(0, ta, sa1, ra1)
    ring(1, 1)
    gathered(2)
    product(2, 0)
    ring(0, 2)
    sum2(0, ta, ra1, sa2, ra2)
    ring(1, 2)
    product(2, 1)
    ring(0, 3)
    first_part()
    cores(2)
    part(2)
    low1(0)
    ring(2, 1)
    gathered(3)
    product(3, 0)
    ring(0, 4)
    ring(1, 3)
    product(3, 1)
    sum3(0, ra2, ra3)
    cores(3)
    part(3)
    low1(1)
    ring(3, 1)
    ring(2, 2)
    low2(0)
    fixed_part()
    ring(0, 5)
    ring(1, 4)
    low2(1)
    first_corner()
    ring(2, 3)
    ring(3, 2)
    ring(1, 5)
    first_rows()
    low3(0)
    ring(2, 4)
    ring(3, 3)
    low3(1)
    swap(0, ga, gca)
    ring(2, 5)
    ring(3, 4)
    low4(0)
    low4(1)
    first_done()
    low5(0)
    ring(3, 5)
    second_rows()

    for s in range(CHUNKS):
        for h in range(2):
            wait(raw.at[0, pl.ds(0, 15 * BLK)], ags_sem.at[s, h])
        wait(csnd.at[s], cs_sem.at[s])
        wait(rsnd.at[s], rs_sem.at[s])
    for p in range(2):
        wait(zg.at[p, pl.ds(0, 7)], zs_sem.at[p])
    for q, s1, s2, r3, g_ in ((0, sa1, sa2, ra3, ga),):
        wait(s1, ars_sem.at[q, 0])
        wait(s2.at[pl.ds(0, 15)], ars_sem.at[q, 1])
        wait(r3.at[pl.ds(0, 7)], ars_sem.at[q, 2])
        wait(g_.at[pl.ds(0, 15)], ars_sem.at[q, 3])
        wait(g_, ars_sem.at[q, 4])
    for c in range(2):
        wait(sb.at[c, pl.ds(0, 15)], bs_sem.at[c, 0])
        wait(rc.at[c, pl.ds(0, 15)], bs_sem.at[c, 1])
        wait(gb.at[c, pl.ds(0, 15)], bs_sem.at[c, 2])
        wait(gb.at[c], bs_sem.at[c, 3])
    low5(1)


def hand_out(*refs):
    for i in range(5):
        refs[5 + i][...] = refs[i][...]


def on_device(known_inverse, pattern, panel_one, panel_two, panel_top, structure, diag_one, diag_two):
    vm, sm, hbm = (pl.BlockSpec(memory_space=s) for s in (pltpu.VMEM, pltpu.SMEM, pl.ANY))
    V, S = pltpu.VMEM, pltpu.SemaphoreType.DMA

    def sums(n, no):
        return [
            V((n, W, W), F32),
            V((n, 256, W), BF), V((n, 256, W), BF),
            V((16, n, 16, W), BF), V((16, n, 16, W), BF),
            V((8, n, 16, W), BF),
            V((16, no, 16, W), BF), V((16, no, 16, W), BF),
        ]

    corner = jax.ShapeDtypeStruct((W, W), BF)
    rows = jax.ShapeDtypeStruct((BLK, W), BF)
    parts = pl.pallas_call(
        kernel,
        out_shape=(rows, corner, corner, rows, corner),
        in_specs=[hbm, sm, vm, vm, vm, vm, vm, vm],
        out_specs=(vm,) * 5,
        scratch_shapes=[
            V((16, 2048, BLK), BF), V((2048, BLK), F32), V((2048, 2048), BF),
            V((CHUNKS, 2, 4, 4, BLK, HALF), BF), V((2, 8, BLK, W), BF),
            V((CHUNKS, 8, BLK, WIDE), F32), V((CHUNKS, 8, BLK, WIDE), BF), V((CHUNKS, 8, BLK, WIDE), BF),
            V((CHUNKS, 2, 7, BLK, HALF), BF), V((CHUNKS, 2, 7, BLK, HALF), BF),
            V((CHUNKS, 2, BLK, HALF), F32), V((W, W), F32),
            *sums(2, 2),
            V((2, W, WIDE), F32), V((2, 16, 2, 16, WIDE), BF), V((2, 16, 2, 16, WIDE), BF),
            V((2, 2, 16, WIDE), BF), V((2, 16, 16, WIDE), BF), V((2, 16, 16, WIDE), BF), V((2, 16, 16, WIDE), BF),
            S((16,)), S((CHUNKS, 2)), S((CHUNKS, 2, 2)), S((CHUNKS, 2)), S((CHUNKS, 2)),
            S((2, 2, 4)), S((2,)),
            S((CHUNKS,)), S((CHUNKS,)), S((CHUNKS, 2, 4)), S((CHUNKS,)), S((1, 5)), S((1, 5)),
            S((2, 4)), S((2, 4)),
        ],
        compiler_params=pltpu.CompilerParams(
            collective_id=0, has_side_effects=True, vmem_limit_bytes=60 * 2**20
        ),
        cost_estimate=pl.CostEstimate(flops=2 * 2048 * 2048 * 1024, bytes_accessed=12 * 2**20, transcendentals=0),
        name="inverse",
    )(
        known_inverse.reshape(16, 2048, BLK),
        pattern.reshape(16, 16),
        panel_one, panel_two, panel_top, structure.reshape(1, BLK), diag_one, diag_two,
    )
    return pl.pallas_call(
        hand_out,
        out_shape=(rows, corner, corner, rows, corner),
        in_specs=[vm] * 5,
        out_specs=(vm,) * 5,
        name="hand_out",
    )(*parts)


def solution(mesh):
    in_specs = (
        P("prow", None, "pcol", None), P("prow", None, "pcol", None),
        P(("prow", "pcol"), None), P(("prow", "pcol"), None),
        P(), P(("prow", "pcol")), P(), P(),
    )
    out_specs = (P(("prow", "pcol"), None), P(), P(), P(("prow", "pcol"), None), P())
    return jax.shard_map(on_device, mesh=mesh, in_specs=in_specs, out_specs=out_specs, check_vma=False)
```

```python
import jax
import jax.numpy as jnp
from jax import lax
from jax.experimental import pallas as pl
from jax.experimental.pallas import tpu as pltpu
from jax.sharding import PartitionSpec as P

MESH = pl.DeviceIdType.MESH
BF = jnp.bfloat16
F32 = jnp.float32
CHUNKS = 4
HALF = 128
WIDE = 256
BLK = 128
W = 512


def dot(a, b):
    return jnp.dot(a, b, preferred_element_type=F32)


def dot_t(a, b):
    return lax.dot_general(a, b, (((0,), (0,)), ((), ())), preferred_element_type=F32)


def kernel(
    m_hbm, pat, p1, p2, ptop, struct, d1, d2,
    o_inv1, o_c1, o_top, o_inv2, o_c2,
    raw, tall, ms, g, zg, keep, csnd, crcv, rsnd, rrcv, red, base,
    ta, sa1, ra1, sa2, ra2, ra3, ga, gca,
    tb, sb, rb, sc, rc, gb, gcb,
    m_sem, ag1_sem, ag2_sem, agf_sem, ags_sem, zg_sem, zs_sem, c_sem, cs_sem, r_sem, rs_sem, ar_sem, ars_sem, br_sem, bs_sem,
):
    me_r = lax.axis_index("prow")
    me_c = lax.axis_index("pcol")
    x, y, z, k = me_r // 4, me_r % 4, me_c // 2, me_c % 2
    other = 1 - k

    def at(dx, dy, dz, dk):
        return (
            ((x + dx) % 4) * 4 + (y + dy) % 4,
            ((z + dz) % 8) * 2 + (k + dk) % 2,
        )

    plane = [(dx, dy, 0, 0) for dx in range(4) for dy in range(4) if dx or dy]
    column = [(0, 0, dz, 0) for dz in range(1, 8)]
    mate = [(0, 0, 0, 1)]
    tower = [(0, 0, dz, dk) for dk in (0, 1) for dz in range(8) if dz or dk]

    def send(src, dst, ssem, rsem, off):
        pltpu.make_async_remote_copy(
            src_ref=src, dst_ref=dst, send_sem=ssem, recv_sem=rsem,
            device_id=at(*off), device_id_type=MESH,
        ).start()

    def wait(ref, sem):
        pltpu.make_async_copy(ref, ref, sem).wait()

    def row_block(i):
        return 2 * i + other if i < 8 else 2 * (i - 8) + k

    for i in range(16):
        pltpu.make_async_copy(m_hbm.at[row_block(i)], raw.at[i], m_sem.at[i]).start()

    barrier = pltpu.get_barrier_semaphore()
    peers = plane + tower
    for off in peers:
        pl.semaphore_signal(barrier, inc=1, device_id=at(*off), device_id_type=MESH)

    flags = jnp.broadcast_to(struct[...], (BLK, BLK)) > 0
    eye = lax.broadcasted_iota(jnp.int32, (BLK, BLK), 0) == lax.broadcasted_iota(
        jnp.int32, (BLK, BLK), 1
    )
    pick = jnp.where(flags & eye, 1.0, 0.0).astype(BF)
    zg[0, z] = p1[...]
    zg[1, z] = dot(pick, p2[...]).astype(BF)
    for s in range(2):
        for h in range(2):
            c0 = s * WIDE + h * HALF
            g[s, h, x, y] = p1[:, c0 : c0 + HALF]

    pl.semaphore_wait(barrier, len(peers))

    def step_along(h, first):
        along_x = (h == 0) == first
        return (lambda d: (d, 0, 0, 0)) if along_x else (lambda d: (0, d, 0, 0))

    def gather1(s):
        for h in range(2):
            off = step_along(h, True)
            blk = g.at[s, h, x, y]
            for d in (1, 3, 2):
                send(blk, blk, ags_sem.at[s, h], ag1_sem.at[s, h], off(d))

    def line(s, h, d, lo, n):
        if h == 0:
            return g.at[s, h, pl.ds(lo, n), (y + d) % 4]
        return g.at[s, h, (x + d) % 4, pl.ds(lo, n)]

    def gather2(s):
        for h in range(2):
            wait(line(s, h, 0, 0, 3), ag1_sem.at[s, h])
            off = step_along(h, False)
            mine = line(s, h, 0, 0, 4)
            send(mine, mine, ags_sem.at[s, h], ag2_sem.at[s, h, 0], off(1))
            send(mine, mine, ags_sem.at[s, h], ag2_sem.at[s, h, 1], off(3))

    def gather3(s):
        for h in range(2):
            off = step_along(h, False)
            wait(line(s, h, 3, 0, 4), ag2_sem.at[s, h, 0])
            low = line(s, h, 3, 0, 2)
            send(low, low, ags_sem.at[s, h], agf_sem.at[s, h], off(1))
            wait(line(s, h, 1, 0, 4), ag2_sem.at[s, h, 1])
            high = line(s, h, 1, 2, 2)
            send(high, high, ags_sem.at[s, h], agf_sem.at[s, h], off(3))

    def gathered(s):
        for h in range(2):
            wait(line(s, h, 2, 0, 4), agf_sem.at[s, h])

    def second_panel():
        v = zg[1, z].astype(F32) - dot(p1[...], ptop[...])
        for s in range(2, CHUNKS):
            for h in range(2):
                c0 = (s - 2) * WIDE + h * HALF
                g[s, h, x, y] = v[:, c0 : c0 + HALF].astype(BF)

    def rows_along(t, p):
        for way in range(2):
            d = t - 1 if way else -(t - 1)
            blk = zg.at[p, (z + d + 8) % 8]
            half = blk.at[pl.ds(64 * way, 64)]
            if t > 1:
                got = half if t == 5 else blk
                wait(got, zg_sem.at[p, way, t - 2])
            if t == 5:
                continue
            src = half if t == 4 else blk
            send(src, src, zs_sem.at[p], zg_sem.at[p, way, t - 1], (0, 0, 7 if way else 1, 0))

    def relayout(lo, hi):
        @pl.loop(lo, hi)
        def _(i):
            rb = jnp.where(i < 8, 2 * i + other, 2 * (i - 8) + k)
            pltpu.make_async_copy(m_hbm.at[rb], raw.at[i], m_sem.at[i]).wait()
            tall[...] = raw[i].astype(F32)
            for a in range(16):
                v = tall[pl.ds(a, BLK, stride=16), :]
                v = jnp.where(pat[rb, a] > 0, v, 0.0)
                ms[pl.ds(i * BLK, BLK), a * BLK : (a + 1) * BLK] = v.astype(BF)

    def panel(s):
        return jnp.concatenate([g[s, h].reshape(2048, HALF) for h in range(2)], axis=1)

    def product(s, tile):
        acc = dot(ms[tile * 1024 : (tile + 1) * 1024, :], panel(s)).reshape(8, BLK, WIDE)
        if tile == 0:
            csnd[s] = acc.astype(BF)
            send(csnd.at[s], crcv.at[s], cs_sem.at[s], c_sem.at[s], mate[0])
        else:
            keep[s] = acc

    def cores(s):
        wait(crcv.at[s], c_sem.at[s])
        keep[s] = keep[s] + crcv[s].astype(F32)

    def part(s):
        v = keep[s].astype(BF).reshape(1024, WIDE)
        c = slice((s % 2) * WIDE, (s % 2 + 1) * WIDE)
        two = zg[1].reshape(1024, W)
        if s < 2:
            ta[0, :, c] = dot_t(zg[0].reshape(1024, W), v)
            ta[1, c, :] = dot_t(v, two)
        else:
            tb[s - 2] = tb[s - 2] + dot_t(two, v)

    def own(s, b, h):
        c = slice(h * HALF, (h + 1) * HALF)
        return keep[s, b, :, c]

    def slots(t):
        return (0, 1) if t == 1 else (2 * t - 3, 2)

    def ring(s, t):
        for way in range(2):
            if t > 1:
                lo, n = slots(t - 1)
                wait(rrcv.at[s, way, pl.ds(lo, n)], r_sem.at[s, way, t - 2])
        if t == 5:
            for h in range(2):
                red[s, h] = own(s, z, h) + rrcv[s, 0, 5 + h].astype(F32) + rrcv[s, 1, 5 + h].astype(F32)
            return
        for way in range(2):
            d = 5 - t if way == 0 else 8 - (5 - t)
            b = (z + d) % 8
            lo, n = slots(t)
            for h in range(2):
                if t == 1:
                    if h == way:
                        rsnd[s, way, 0] = own(s, b, h).astype(BF)
                    continue
                v = own(s, b, h)
                if t > 2:
                    v = v + rrcv[s, way, slots(t - 1)[0] + h].astype(F32)
                elif h == way:
                    v = v + rrcv[s, way, 0].astype(F32)
                rsnd[s, way, lo + h] = v.astype(BF)
            send(
                rsnd.at[s, way, pl.ds(lo, n)], rrcv.at[s, way, pl.ds(lo, n)],
                rs_sem.at[s], r_sem.at[s, way, t - 1], (0, 0, 1 if way == 0 else 7, 0),
            )

    def sum1(q, t32, s1, r1):
        s1[...] = t32[:, pl.ds(pl.multiple_of(other * 256, 256), 256), :].astype(BF)
        send(s1, r1, ars_sem.at[q, 0], ar_sem.at[q, 0], mate[0])

    def sum2(q, t32, r1, s2, r2):
        wait(r1, ar_sem.at[q, 0])
        n = t32.shape[0]
        for m in range(n):
            v = t32[m, pl.ds(pl.multiple_of(k * 256, 256), 256), :] + r1[m].astype(F32)
            s2[:, m] = v.astype(BF).reshape(16, 16, W)
        for off in plane:
            j = ((x + off[0]) % 4) * 4 + (y + off[1]) % 4
            send(s2.at[j], r2.at[me_r], ars_sem.at[q, 1], ar_sem.at[q, 1], off)
        r2[me_r] = s2[me_r]

    def sum3(q, r2, r3):
        wait(r2.at[pl.ds(0, 15)], ar_sem.at[q, 1])
        v = r2[0].astype(F32)
        for j in range(1, 16):
            v = v + r2[j].astype(F32)
        r3[z] = v.astype(BF)
        for off in column:
            send(r3.at[z], r3.at[z], ars_sem.at[q, 2], ar_sem.at[q, 2], off)

    def sum4(q, r3):
        wait(r3.at[pl.ds(0, 7)], ar_sem.at[q, 2])
        v = r3[0].astype(F32)
        for j in range(1, 8):
            v = v + r3[j].astype(F32)
        return v

    def spread(q, ga_):
        for off in plane:
            send(ga_.at[me_r], ga_.at[me_r], ars_sem.at[q, 3], ar_sem.at[q, 3], off)

    def swap(q, ga_, gc_):
        wait(ga_.at[pl.ds(0, 15)], ar_sem.at[q, 3])
        send(ga_, gc_, ars_sem.at[q, 4], ar_sem.at[q, 4], mate[0])

    def lay(out, ga_, gc_, m):
        out[pl.ds(pl.multiple_of(k * 256, 256), 256), :] = ga_[:, m].reshape(256, W)
        out[pl.ds(pl.multiple_of(other * 256, 256), 256), :] = gc_[:, m].reshape(256, W)

    my_rows = pl.ds(pl.multiple_of(k * 256 + me_r * 16, 16), 16)

    def first_rows():
        r = jnp.concatenate(
            [jnp.concatenate([red[s, h] for h in range(2)], axis=1) for s in range(2)], axis=1
        )
        o_inv1[...] = (-r).astype(BF)

    def second_rows():
        r = jnp.concatenate(
            [jnp.concatenate([red[s, h] for h in range(2)], axis=1) for s in range(2, 4)], axis=1
        )
        kept = dot(pick, jnp.ones((BLK, W), BF)) > 0.5
        o_inv2[...] = jnp.where(kept, -r, 0.0).astype(BF)

    def first_corner():
        v = sum4(0, ra3)
        s1 = d1[my_rows, :].astype(F32) + v[0]
        hi = s1.astype(BF)
        rest = s1 - hi.astype(F32)
        mid = rest.astype(BF)
        low = (rest - mid.astype(F32)).astype(BF)
        t = ptop[...]
        top = dot(hi, t) + (dot(mid, t) + dot(low, t))
        ga[me_r, 0] = hi
        ga[me_r, 1] = (v[1] - top).astype(BF)
        spread(0, ga)

    def first_done():
        wait(gca, ar_sem.at[0, 4])
        lay(o_c1, ga, gca, 0)
        lay(o_top, ga, gca, 1)

    def fixed_part():
        t = ptop[...]
        base[...] = d2[...].astype(F32) + dot_t(t, dot(d1[...], t).astype(BF))

    def first_part():
        t = ptop[...]
        u = dot_t(t, (dot(ta[0].astype(BF), t) - ta[1]).astype(BF))
        tb[0] = u[:, :WIDE]
        tb[1] = u[:, WIDE:]

    def low1(c):
        for half in range(2):
            sb[c, :, half] = tb[c, half * 256 : (half + 1) * 256].astype(BF).reshape(16, 16, WIDE)
        for off in plane:
            j = ((x + off[0]) % 4) * 4 + (y + off[1]) % 4
            send(sb.at[c, j], rb.at[c, me_r], bs_sem.at[c, 0], br_sem.at[c, 0], off)
        rb[c, me_r] = sb[c, me_r]

    def low2(c):
        wait(rb.at[c, pl.ds(0, 15)], br_sem.at[c, 0])
        v = rb[c, 0].astype(F32)
        for j in range(1, 16):
            v = v + rb[c, j].astype(F32)
        sc[c] = v.astype(BF)
        for off in tower:
            to = k if off[3] == 0 else other
            send(sc.at[c, to], rc.at[c, me_c], bs_sem.at[c, 1], br_sem.at[c, 1], off)
        rc[c, me_c] = sc[c, k]

    def low3(c):
        wait(rc.at[c, pl.ds(0, 15)], br_sem.at[c, 1])
        v = base[my_rows, c * WIDE : (c + 1) * WIDE]
        for j in range(16):
            v = v + rc[c, j].astype(F32)
        gb[c, me_r] = v.astype(BF)
        for off in plane:
            send(gb.at[c, me_r], gb.at[c, me_r], bs_sem.at[c, 2], br_sem.at[c, 2], off)

    def low4(c):
        wait(gb.at[c, pl.ds(0, 15)], br_sem.at[c, 2])
        send(gb.at[c], gcb.at[c], bs_sem.at[c, 3], br_sem.at[c, 3], mate[0])

    def low5(c):
        wait(gcb.at[c], br_sem.at[c, 3])
        cols = slice(c * WIDE, (c + 1) * WIDE)
        o_c2[pl.ds(pl.multiple_of(k * 256, 256), 256), cols] = gb[c].reshape(256, WIDE)
        o_c2[pl.ds(pl.multiple_of(other * 256, 256), 256), cols] = gcb[c].reshape(256, WIDE)

    gather1(0)
    rows_along(1, 0)
    gather1(1)
    second_panel()
    rows_along(1, 1)
    gather1(2)
    relayout(0, 4)
    gather2(0)
    gather1(3)
    rows_along(2, 0)
    relayout(4, 6)
    gather2(1)
    rows_along(2, 1)
    relayout(6, 12)
    rows_along(3, 0)
    gather3(0)
    gather2(2)
    relayout(12, 16)
    gather3(1)
    gather2(3)
    rows_along(3, 1)
    gathered(0)
    product(0, 0)
    product(0, 1)
    rows_along(4, 0)
    rows_along(4, 1)
    gather3(2)
    gathered(1)
    product(1, 0)
    gather3(3)
    cores(0)
    ring(0, 1)
    product(1, 1)
    rows_along(5, 0)
    rows_along(5, 1)
    part(0)
    cores(1)
    part(1)
    sum1(0, ta, sa1, ra1)
    ring(1, 1)
    gathered(2)
    product(2, 0)
    ring(0, 2)
    sum2(0, ta, ra1, sa2, ra2)
    product(2, 1)
    ring(0, 3)
    ring(1, 2)
    first_part()
    gathered(3)
    product(3, 0)
    cores(2)
    part(2)
    low1(0)
    ring(2, 1)
    ring(0, 4)
    ring(1, 3)
    product(3, 1)
    cores(3)
    part(3)
    low1(1)
    ring(3, 1)
    ring(2, 2)
    sum3(0, ra2, ra3)
    low2(0)
    fixed_part()
    ring(0, 5)
    ring(1, 4)
    low2(1)
    ring(2, 3)
    ring(3, 2)
    first_corner()
    low3(0)
    ring(1, 5)
    first_rows()
    ring(2, 4)
    ring(3, 3)
    low3(1)
    swap(0, ga, gca)
    ring(2, 5)
    ring(3, 4)
    low4(0)
    low4(1)
    first_done()
    low5(0)
    ring(3, 5)
    second_rows()

    for s in range(CHUNKS):
        for h in range(2):
            wait(raw.at[0, pl.ds(0, 15 * BLK)], ags_sem.at[s, h])
        wait(csnd.at[s], cs_sem.at[s])
        wait(rsnd.at[s], rs_sem.at[s])
    for p in range(2):
        wait(zg.at[p, pl.ds(0, 7)], zs_sem.at[p])
    for q, s1, s2, r3, g_ in ((0, sa1, sa2, ra3, ga),):
        wait(s1, ars_sem.at[q, 0])
        wait(s2.at[pl.ds(0, 15)], ars_sem.at[q, 1])
        wait(r3.at[pl.ds(0, 7)], ars_sem.at[q, 2])
        wait(g_.at[pl.ds(0, 15)], ars_sem.at[q, 3])
        wait(g_, ars_sem.at[q, 4])
    for c in range(2):
        wait(sb.at[c, pl.ds(0, 15)], bs_sem.at[c, 0])
        wait(rc.at[c, pl.ds(0, 15)], bs_sem.at[c, 1])
        wait(gb.at[c, pl.ds(0, 15)], bs_sem.at[c, 2])
        wait(gb.at[c], bs_sem.at[c, 3])
    low5(1)


def hand_out(*refs):
    for i in range(5):
        refs[5 + i][...] = refs[i][...]


def on_device(known_inverse, pattern, panel_one, panel_two, panel_top, structure, diag_one, diag_two):
    vm, sm, hbm = (pl.BlockSpec(memory_space=s) for s in (pltpu.VMEM, pltpu.SMEM, pl.ANY))
    V, S = pltpu.VMEM, pltpu.SemaphoreType.DMA

    def sums(n, no):
        return [
            V((n, W, W), F32),
            V((n, 256, W), BF), V((n, 256, W), BF),
            V((16, n, 16, W), BF), V((16, n, 16, W), BF),
            V((8, n, 16, W), BF),
            V((16, no, 16, W), BF), V((16, no, 16, W), BF),
        ]

    corner = jax.ShapeDtypeStruct((W, W), BF)
    rows = jax.ShapeDtypeStruct((BLK, W), BF)
    parts = pl.pallas_call(
        kernel,
        out_shape=(rows, corner, corner, rows, corner),
        in_specs=[hbm, sm, vm, vm, vm, vm, vm, vm],
        out_specs=(vm,) * 5,
        scratch_shapes=[
            V((16, 2048, BLK), BF), V((2048, BLK), F32), V((2048, 2048), BF),
            V((CHUNKS, 2, 4, 4, BLK, HALF), BF), V((2, 8, BLK, W), BF),
            V((CHUNKS, 8, BLK, WIDE), F32), V((CHUNKS, 8, BLK, WIDE), BF), V((CHUNKS, 8, BLK, WIDE), BF),
            V((CHUNKS, 2, 7, BLK, HALF), BF), V((CHUNKS, 2, 7, BLK, HALF), BF),
            V((CHUNKS, 2, BLK, HALF), F32), V((W, W), F32),
            *sums(2, 2),
            V((2, W, WIDE), F32), V((2, 16, 2, 16, WIDE), BF), V((2, 16, 2, 16, WIDE), BF),
            V((2, 2, 16, WIDE), BF), V((2, 16, 16, WIDE), BF), V((2, 16, 16, WIDE), BF), V((2, 16, 16, WIDE), BF),
            S((16,)), S((CHUNKS, 2)), S((CHUNKS, 2, 2)), S((CHUNKS, 2)), S((CHUNKS, 2)),
            S((2, 2, 4)), S((2,)),
            S((CHUNKS,)), S((CHUNKS,)), S((CHUNKS, 2, 4)), S((CHUNKS,)), S((1, 5)), S((1, 5)),
            S((2, 4)), S((2, 4)),
        ],
        compiler_params=pltpu.CompilerParams(
            collective_id=0, has_side_effects=True, vmem_limit_bytes=60 * 2**20
        ),
        cost_estimate=pl.CostEstimate(flops=2 * 2048 * 2048 * 1024, bytes_accessed=12 * 2**20, transcendentals=0),
        name="inverse",
    )(
        known_inverse.reshape(16, 2048, BLK),
        pattern.reshape(16, 16),
        panel_one, panel_two, panel_top, structure.reshape(1, BLK), diag_one, diag_two,
    )
    return pl.pallas_call(
        hand_out,
        out_shape=(rows, corner, corner, rows, corner),
        in_specs=[vm] * 5,
        out_specs=(vm,) * 5,
        name="hand_out",
    )(*parts)


def solution(mesh):
    in_specs = (
        P("prow", None, "pcol", None), P("prow", None, "pcol", None),
        P(("prow", "pcol"), None), P(("prow", "pcol"), None),
        P(), P(("prow", "pcol")), P(), P(),
    )
    out_specs = (P(("prow", "pcol"), None), P(), P(), P(("prow", "pcol"), None), P())
    return jax.shard_map(on_device, mesh=mesh, in_specs=in_specs, out_specs=out_specs, check_vma=False)
```

```python
import jax
import jax.numpy as jnp
from jax import lax
from jax.experimental import pallas as pl
from jax.experimental.pallas import tpu as pltpu
from jax.sharding import PartitionSpec as P

MESH = pl.DeviceIdType.MESH
BF = jnp.bfloat16
F32 = jnp.float32
CHUNKS = 4
HALF = 128
WIDE = 256
BLK = 128
W = 512


def dot(a, b):
    return jnp.dot(a, b, preferred_element_type=F32)


def dot_t(a, b):
    return lax.dot_general(a, b, (((0,), (0,)), ((), ())), preferred_element_type=F32)


def kernel(
    m_hbm, pat, p1, p2, ptop, struct, d1, d2,
    o_inv1, o_c1, o_top, o_inv2, o_c2,
    raw, tall, ms, g, zg, keep, csnd, crcv, rsnd, rrcv, red, base,
    ta, sa1, ra1, sa2, ra2, ra3, ga, gca,
    tb, sb, rb, sc, rc, gb, gcb,
    m_sem, ag1_sem, ag2_sem, agf_sem, ags_sem, zg_sem, zs_sem, c_sem, cs_sem, r_sem, rs_sem, ar_sem, ars_sem, br_sem, bs_sem,
):
    me_r = lax.axis_index("prow")
    me_c = lax.axis_index("pcol")
    x, y, z, k = me_r // 4, me_r % 4, me_c // 2, me_c % 2
    other = 1 - k

    def at(dx, dy, dz, dk):
        return (
            ((x + dx) % 4) * 4 + (y + dy) % 4,
            ((z + dz) % 8) * 2 + (k + dk) % 2,
        )

    plane = [(dx, dy, 0, 0) for dx in range(4) for dy in range(4) if dx or dy]
    column = [(0, 0, dz, 0) for dz in range(1, 8)]
    mate = [(0, 0, 0, 1)]
    tower = [(0, 0, dz, dk) for dk in (0, 1) for dz in range(8) if dz or dk]

    def send(src, dst, ssem, rsem, off):
        pltpu.make_async_remote_copy(
            src_ref=src, dst_ref=dst, send_sem=ssem, recv_sem=rsem,
            device_id=at(*off), device_id_type=MESH,
        ).start()

    def wait(ref, sem):
        pltpu.make_async_copy(ref, ref, sem).wait()

    def row_block(i):
        return 2 * i + other if i < 8 else 2 * (i - 8) + k

    for i in range(16):
        pltpu.make_async_copy(m_hbm.at[row_block(i)], raw.at[i], m_sem.at[i]).start()

    barrier = pltpu.get_barrier_semaphore()
    peers = [o for o in plane if 0 in o[:2]] + [(0, 0, 1, 0), (0, 0, 7, 0)] + mate
    for off in peers:
        pl.semaphore_signal(barrier, inc=1, device_id=at(*off), device_id_type=MESH)

    flags = jnp.broadcast_to(struct[...], (BLK, BLK)) > 0
    eye = lax.broadcasted_iota(jnp.int32, (BLK, BLK), 0) == lax.broadcasted_iota(
        jnp.int32, (BLK, BLK), 1
    )
    pick = jnp.where(flags & eye, 1.0, 0.0).astype(BF)
    zg[0, z] = p1[...]
    zg[1, z] = dot(pick, p2[...]).astype(BF)
    for s in range(2):
        for h in range(2):
            c0 = s * WIDE + h * HALF
            g[s, h, x, y] = p1[:, c0 : c0 + HALF]

    pl.semaphore_wait(barrier, len(peers))

    def step_along(h, first):
        along_x = (h == 0) == first
        return (lambda d: (d, 0, 0, 0)) if along_x else (lambda d: (0, d, 0, 0))

    def gather1(s):
        for h in range(2):
            off = step_along(h, True)
            blk = g.at[s, h, x, y]
            for d in (1, 3, 2):
                send(blk, blk, ags_sem.at[s, h], ag1_sem.at[s, h], off(d))

    def line(s, h, d, lo, n):
        if h == 0:
            return g.at[s, h, pl.ds(lo, n), (y + d) % 4]
        return g.at[s, h, (x + d) % 4, pl.ds(lo, n)]

    def gather2(s):
        for h in range(2):
            wait(line(s, h, 0, 0, 3), ag1_sem.at[s, h])
            off = step_along(h, False)
            mine = line(s, h, 0, 0, 4)
            send(mine, mine, ags_sem.at[s, h], ag2_sem.at[s, h, 0], off(1))
            send(mine, mine, ags_sem.at[s, h], ag2_sem.at[s, h, 1], off(3))

    def gather3(s):
        for h in range(2):
            off = step_along(h, False)
            wait(line(s, h, 3, 0, 4), ag2_sem.at[s, h, 0])
            low = line(s, h, 3, 0, 2)
            send(low, low, ags_sem.at[s, h], agf_sem.at[s, h], off(1))
            wait(line(s, h, 1, 0, 4), ag2_sem.at[s, h, 1])
            high = line(s, h, 1, 2, 2)
            send(high, high, ags_sem.at[s, h], agf_sem.at[s, h], off(3))

    def gathered(s):
        for h in range(2):
            wait(line(s, h, 2, 0, 4), agf_sem.at[s, h])

    def second_panel():
        v = zg[1, z].astype(F32) - dot(p1[...], ptop[...])
        for s in range(2, CHUNKS):
            for h in range(2):
                c0 = (s - 2) * WIDE + h * HALF
                g[s, h, x, y] = v[:, c0 : c0 + HALF].astype(BF)

    def rows_along(t, p):
        for way in range(2):
            d = t - 1 if way else -(t - 1)
            blk = zg.at[p, (z + d + 8) % 8]
            half = blk.at[pl.ds(64 * way, 64)]
            if t > 1:
                got = half if t == 5 else blk
                wait(got, zg_sem.at[p, way, t - 2])
            if t == 5:
                continue
            src = half if t == 4 else blk
            send(src, src, zs_sem.at[p], zg_sem.at[p, way, t - 1], (0, 0, 7 if way else 1, 0))

    def relayout(lo, hi):
        @pl.loop(lo, hi)
        def _(i):
            rb = jnp.where(i < 8, 2 * i + other, 2 * (i - 8) + k)
            pltpu.make_async_copy(m_hbm.at[rb], raw.at[i], m_sem.at[i]).wait()
            tall[...] = raw[i].astype(F32)
            for a in range(16):
                v = tall[pl.ds(a, BLK, stride=16), :]
                v = jnp.where(pat[rb, a] > 0, v, 0.0)
                ms[pl.ds(i * BLK, BLK), a * BLK : (a + 1) * BLK] = v.astype(BF)

    def panel(s):
        return jnp.concatenate([g[s, h].reshape(2048, HALF) for h in range(2)], axis=1)

    def product(s, tile):
        acc = dot(ms[tile * 1024 : (tile + 1) * 1024, :], panel(s)).reshape(8, BLK, WIDE)
        if tile == 0:
            csnd[s] = acc.astype(BF)
            send(csnd.at[s], crcv.at[s], cs_sem.at[s], c_sem.at[s], mate[0])
        else:
            keep[s] = acc

    def cores(s):
        wait(crcv.at[s], c_sem.at[s])
        keep[s] = keep[s] + crcv[s].astype(F32)

    def part(s):
        v = keep[s].astype(BF).reshape(1024, WIDE)
        c = slice((s % 2) * WIDE, (s % 2 + 1) * WIDE)
        two = zg[1].reshape(1024, W)
        if s < 2:
            ta[0, :, c] = dot_t(zg[0].reshape(1024, W), v)
            ta[1, c, :] = dot_t(v, two)
        else:
            tb[s - 2] = tb[s - 2] + dot_t(two, v)

    def own(s, b, h):
        c = slice(h * HALF, (h + 1) * HALF)
        return keep[s, b, :, c]

    def slots(t):
        return (0, 1) if t == 1 else (2 * t - 3, 2)

    def ring(s, t):
        for way in range(2):
            if t > 1:
                lo, n = slots(t - 1)
                wait(rrcv.at[s, way, pl.ds(lo, n)], r_sem.at[s, way, t - 2])
        if t == 5:
            for h in range(2):
                red[s, h] = own(s, z, h) + rrcv[s, 0, 5 + h].astype(F32) + rrcv[s, 1, 5 + h].astype(F32)
            return
        for way in range(2):
            d = 5 - t if way == 0 else 8 - (5 - t)
            b = (z + d) % 8
            lo, n = slots(t)
            for h in range(2):
                if t == 1:
                    if h == way:
                        rsnd[s, way, 0] = own(s, b, h).astype(BF)
                    continue
                v = own(s, b, h)
                if t > 2:
                    v = v + rrcv[s, way, slots(t - 1)[0] + h].astype(F32)
                elif h == way:
                    v = v + rrcv[s, way, 0].astype(F32)
                rsnd[s, way, lo + h] = v.astype(BF)
            send(
                rsnd.at[s, way, pl.ds(lo, n)], rrcv.at[s, way, pl.ds(lo, n)],
                rs_sem.at[s], r_sem.at[s, way, t - 1], (0, 0, 1 if way == 0 else 7, 0),
            )

    def sum1(q, t32, s1, r1):
        s1[...] = t32[:, pl.ds(pl.multiple_of(other * 256, 256), 256), :].astype(BF)
        send(s1, r1, ars_sem.at[q, 0], ar_sem.at[q, 0], mate[0])

    def sum2(q, t32, r1, s2, r2):
        wait(r1, ar_sem.at[q, 0])
        n = t32.shape[0]
        for m in range(n):
            v = t32[m, pl.ds(pl.multiple_of(k * 256, 256), 256), :] + r1[m].astype(F32)
            s2[:, m] = v.astype(BF).reshape(16, 16, W)
        for off in plane:
            j = ((x + off[0]) % 4) * 4 + (y + off[1]) % 4
            send(s2.at[j], r2.at[me_r], ars_sem.at[q, 1], ar_sem.at[q, 1], off)
        r2[me_r] = s2[me_r]

    def sum3(q, r2, r3):
        wait(r2.at[pl.ds(0, 15)], ar_sem.at[q, 1])
        v = r2[0].astype(F32)
        for j in range(1, 16):
            v = v + r2[j].astype(F32)
        r3[z] = v.astype(BF)
        for off in column:
            send(r3.at[z], r3.at[z], ars_sem.at[q, 2], ar_sem.at[q, 2], off)

    def sum4(q, r3):
        wait(r3.at[pl.ds(0, 7)], ar_sem.at[q, 2])
        v = r3[0].astype(F32)
        for j in range(1, 8):
            v = v + r3[j].astype(F32)
        return v

    def spread(q, ga_):
        for off in plane:
            send(ga_.at[me_r], ga_.at[me_r], ars_sem.at[q, 3], ar_sem.at[q, 3], off)

    def swap(q, ga_, gc_):
        wait(ga_.at[pl.ds(0, 15)], ar_sem.at[q, 3])
        send(ga_, gc_, ars_sem.at[q, 4], ar_sem.at[q, 4], mate[0])

    def lay(out, ga_, gc_, m):
        out[pl.ds(pl.multiple_of(k * 256, 256), 256), :] = ga_[:, m].reshape(256, W)
        out[pl.ds(pl.multiple_of(other * 256, 256), 256), :] = gc_[:, m].reshape(256, W)

    my_rows = pl.ds(pl.multiple_of(k * 256 + me_r * 16, 16), 16)

    def first_rows():
        r = jnp.concatenate(
            [jnp.concatenate([red[s, h] for h in range(2)], axis=1) for s in range(2)], axis=1
        )
        o_inv1[...] = (-r).astype(BF)

    def second_rows():
        r = jnp.concatenate(
            [jnp.concatenate([red[s, h] for h in range(2)], axis=1) for s in range(2, 4)], axis=1
        )
        kept = dot(pick, jnp.ones((BLK, W), BF)) > 0.5
        o_inv2[...] = jnp.where(kept, -r, 0.0).astype(BF)

    def first_corner():
        v = sum4(0, ra3)
        s1 = d1[my_rows, :].astype(F32) + v[0]
        hi = s1.astype(BF)
        rest = s1 - hi.astype(F32)
        mid = rest.astype(BF)
        low = (rest - mid.astype(F32)).astype(BF)
        t = ptop[...]
        top = dot(hi, t) + (dot(mid, t) + dot(low, t))
        ga[me_r, 0] = hi
        ga[me_r, 1] = (v[1] - top).astype(BF)
        spread(0, ga)

    def first_done():
        wait(gca, ar_sem.at[0, 4])
        lay(o_c1, ga, gca, 0)
        lay(o_top, ga, gca, 1)

    def fixed_part():
        t = ptop[...]
        base[...] = d2[...].astype(F32) + dot_t(t, dot(d1[...], t).astype(BF))

    def first_part():
        t = ptop[...]
        u = dot_t(t, (dot(ta[0].astype(BF), t) - ta[1]).astype(BF))
        tb[0] = u[:, :WIDE]
        tb[1] = u[:, WIDE:]

    def low1(c):
        for half in range(2):
            sb[c, :, half] = tb[c, half * 256 : (half + 1) * 256].astype(BF).reshape(16, 16, WIDE)
        for off in plane:
            j = ((x + off[0]) % 4) * 4 + (y + off[1]) % 4
            send(sb.at[c, j], rb.at[c, me_r], bs_sem.at[c, 0], br_sem.at[c, 0], off)
        rb[c, me_r] = sb[c, me_r]

    def low2(c):
        wait(rb.at[c, pl.ds(0, 15)], br_sem.at[c, 0])
        v = rb[c, 0].astype(F32)
        for j in range(1, 16):
            v = v + rb[c, j].astype(F32)
        sc[c] = v.astype(BF)
        for off in tower:
            to = k if off[3] == 0 else other
            send(sc.at[c, to], rc.at[c, me_c], bs_sem.at[c, 1], br_sem.at[c, 1], off)
        rc[c, me_c] = sc[c, k]

    def low3(c):
        wait(rc.at[c, pl.ds(0, 15)], br_sem.at[c, 1])
        v = base[my_rows, c * WIDE : (c + 1) * WIDE]
        for j in range(16):
            v = v + rc[c, j].astype(F32)
        gb[c, me_r] = v.astype(BF)
        for off in plane:
            send(gb.at[c, me_r], gb.at[c, me_r], bs_sem.at[c, 2], br_sem.at[c, 2], off)

    def low4(c):
        wait(gb.at[c, pl.ds(0, 15)], br_sem.at[c, 2])
        send(gb.at[c], gcb.at[c], bs_sem.at[c, 3], br_sem.at[c, 3], mate[0])

    def low5(c):
        wait(gcb.at[c], br_sem.at[c, 3])
        cols = slice(c * WIDE, (c + 1) * WIDE)
        o_c2[pl.ds(pl.multiple_of(k * 256, 256), 256), cols] = gb[c].reshape(256, WIDE)
        o_c2[pl.ds(pl.multiple_of(other * 256, 256), 256), cols] = gcb[c].reshape(256, WIDE)

    gather1(0)
    rows_along(1, 0)
    gather1(1)
    second_panel()
    rows_along(1, 1)
    gather1(2)
    relayout(0, 4)
    gather2(0)
    gather1(3)
    rows_along(2, 0)
    relayout(4, 6)
    gather2(1)
    rows_along(2, 1)
    relayout(6, 12)
    rows_along(3, 0)
    gather3(0)
    gather2(2)
    relayout(12, 16)
    gather3(1)
    gather2(3)
    rows_along(3, 1)
    gathered(0)
    product(0, 0)
    product(0, 1)
    rows_along(4, 0)
    rows_along(4, 1)
    gather3(2)
    gathered(1)
    product(1, 0)
    gather3(3)
    cores(0)
    ring(0, 1)
    product(1, 1)
    rows_along(5, 0)
    rows_along(5, 1)
    part(0)
    cores(1)
    part(1)
    sum1(0, ta, sa1, ra1)
    ring(1, 1)
    gathered(2)
    product(2, 0)
    ring(0, 2)
    sum2(0, ta, ra1, sa2, ra2)
    product(2, 1)
    ring(0, 3)
    ring(1, 2)
    first_part()
    gathered(3)
    product(3, 0)
    cores(2)
    part(2)
    low1(0)
    ring(2, 1)
    ring(0, 4)
    ring(1, 3)
    product(3, 1)
    cores(3)
    part(3)
    low1(1)
    ring(3, 1)
    ring(2, 2)
    sum3(0, ra2, ra3)
    ring(0, 5)
    ring(1, 4)
    low2(0)
    low2(1)
    fixed_part()
    ring(2, 3)
    ring(3, 2)
    first_corner()
    low3(0)
    ring(1, 5)
    first_rows()
    ring(2, 4)
    ring(3, 3)
    low3(1)
    swap(0, ga, gca)
    ring(2, 5)
    ring(3, 4)
    low4(0)
    low4(1)
    first_done()
    low5(0)
    ring(3, 5)
    second_rows()

    for s in range(CHUNKS):
        for h in range(2):
            wait(raw.at[0, pl.ds(0, 15 * BLK)], ags_sem.at[s, h])
        wait(csnd.at[s], cs_sem.at[s])
        wait(rsnd.at[s], rs_sem.at[s])
    for p in range(2):
        wait(zg.at[p, pl.ds(0, 7)], zs_sem.at[p])
    for q, s1, s2, r3, g_ in ((0, sa1, sa2, ra3, ga),):
        wait(s1, ars_sem.at[q, 0])
        wait(s2.at[pl.ds(0, 15)], ars_sem.at[q, 1])
        wait(r3.at[pl.ds(0, 7)], ars_sem.at[q, 2])
        wait(g_.at[pl.ds(0, 15)], ars_sem.at[q, 3])
        wait(g_, ars_sem.at[q, 4])
    for c in range(2):
        wait(sb.at[c, pl.ds(0, 15)], bs_sem.at[c, 0])
        wait(rc.at[c, pl.ds(0, 15)], bs_sem.at[c, 1])
        wait(gb.at[c, pl.ds(0, 15)], bs_sem.at[c, 2])
        wait(gb.at[c], bs_sem.at[c, 3])
    low5(1)


def hand_out(*refs):
    for i in range(5):
        refs[5 + i][...] = refs[i][...]


def on_device(known_inverse, pattern, panel_one, panel_two, panel_top, structure, diag_one, diag_two):
    vm, sm, hbm = (pl.BlockSpec(memory_space=s) for s in (pltpu.VMEM, pltpu.SMEM, pl.ANY))
    V, S = pltpu.VMEM, pltpu.SemaphoreType.DMA

    def sums(n, no):
        return [
            V((n, W, W), F32),
            V((n, 256, W), BF), V((n, 256, W), BF),
            V((16, n, 16, W), BF), V((16, n, 16, W), BF),
            V((8, n, 16, W), BF),
            V((16, no, 16, W), BF), V((16, no, 16, W), BF),
        ]

    corner = jax.ShapeDtypeStruct((W, W), BF)
    rows = jax.ShapeDtypeStruct((BLK, W), BF)
    parts = pl.pallas_call(
        kernel,
        out_shape=(rows, corner, corner, rows, corner),
        in_specs=[hbm, sm, vm, vm, vm, vm, vm, vm],
        out_specs=(vm,) * 5,
        scratch_shapes=[
            V((16, 2048, BLK), BF), V((2048, BLK), F32), V((2048, 2048), BF),
            V((CHUNKS, 2, 4, 4, BLK, HALF), BF), V((2, 8, BLK, W), BF),
            V((CHUNKS, 8, BLK, WIDE), F32), V((CHUNKS, 8, BLK, WIDE), BF), V((CHUNKS, 8, BLK, WIDE), BF),
            V((CHUNKS, 2, 7, BLK, HALF), BF), V((CHUNKS, 2, 7, BLK, HALF), BF),
            V((CHUNKS, 2, BLK, HALF), F32), V((W, W), F32),
            *sums(2, 2),
            V((2, W, WIDE), F32), V((2, 16, 2, 16, WIDE), BF), V((2, 16, 2, 16, WIDE), BF),
            V((2, 2, 16, WIDE), BF), V((2, 16, 16, WIDE), BF), V((2, 16, 16, WIDE), BF), V((2, 16, 16, WIDE), BF),
            S((16,)), S((CHUNKS, 2)), S((CHUNKS, 2, 2)), S((CHUNKS, 2)), S((CHUNKS, 2)),
            S((2, 2, 4)), S((2,)),
            S((CHUNKS,)), S((CHUNKS,)), S((CHUNKS, 2, 4)), S((CHUNKS,)), S((1, 5)), S((1, 5)),
            S((2, 4)), S((2, 4)),
        ],
        compiler_params=pltpu.CompilerParams(
            collective_id=0, has_side_effects=True, vmem_limit_bytes=60 * 2**20
        ),
        cost_estimate=pl.CostEstimate(flops=2 * 2048 * 2048 * 1024, bytes_accessed=12 * 2**20, transcendentals=0),
        name="inverse",
    )(
        known_inverse.reshape(16, 2048, BLK),
        pattern.reshape(16, 16),
        panel_one, panel_two, panel_top, structure.reshape(1, BLK), diag_one, diag_two,
    )
    return pl.pallas_call(
        hand_out,
        out_shape=(rows, corner, corner, rows, corner),
        in_specs=[vm] * 5,
        out_specs=(vm,) * 5,
        name="hand_out",
    )(*parts)


def solution(mesh):
    in_specs = (
        P("prow", None, "pcol", None), P("prow", None, "pcol", None),
        P(("prow", "pcol"), None), P(("prow", "pcol"), None),
        P(), P(("prow", "pcol")), P(), P(),
    )
    out_specs = (P(("prow", "pcol"), None), P(), P(), P(("prow", "pcol"), None), P())
    return jax.shard_map(on_device, mesh=mesh, in_specs=in_specs, out_specs=out_specs, check_vma=False)
```
